256 devices in a mesh: slab: 8 (over y, core), head: 32 (over z, x).
Axes of the slice: x: 4, y: 4, z: 8, core: 2. Of those that a mesh axis runs over, the one named last changes fastest.
Arguments:
- queries: bfloat16 [32768, 4096], P(('slab', 'head')), may hold values from -500 to 500
- keys: bfloat16 [32768, 4096], P(('slab', 'head')), may hold values from -500 to 500
- values: bfloat16 [32768, 4096], P(('slab', 'head')), may hold values from -6 to 6
- q_gain: float32 [128], replicated, may hold values from 0.25 to 1.75
- k_gain: float32 [128], replicated, may hold values from 0.25 to 1.75
- windows: int32 [32, 3], P('head'), may hold values from 0 to 1, as said below
Outputs:
- attended: bfloat16 [32768, 4096], P(('slab', 'head'))
The draws below stay inside these ranges and needn't reach their ends.
Inputs may be any that keep to these rules, and one draw needn't show every extreme that they name: `windows`: some head has all three extents 1 and some head all three 0.
All inputs are finite; a program needn't handle non-finite values.
Results may differ from the reference program's by a relative error of at most 0.0067.
Values may be sent and summed in bfloat16 or wider, within the bound.
No kernel may reach another device: no remote copies, remote signals or barrier semaphores. Data moves between devices by JAX's collectives and lax.ppermute only.
A program may use at most 192 MiB of HBM per device.

```python
import math
import jax
import jax.numpy as jnp
from jax import lax

HD = 128
TILE = 128
GH = 4
GW = 4
SLAB_TF = 2
HEADS = 32
TOKENS = 32768
N_SLAB = 8


def scaled_field(key):
    keys_split = jax.random.split(key, 5)
    row_count = TOKENS
    column_count = HEADS * HD
    rough_part = jax.random.normal(keys_split[0], (row_count, column_count), jnp.float32)
    values_base = jnp.clip(rough_part, -5.0, 5.0)
    row_scale = 10.0 ** jax.random.uniform(keys_split[3], (row_count, 1), jnp.float32)
    column_scale = 10.0 ** jax.random.uniform(keys_split[4], (1, column_count), jnp.float32)
    return (values_base * row_scale * column_scale).astype(jnp.bfloat16)


def draw_queries(key, part):
    key = jax.random.fold_in(key, 11)
    return scaled_field(key)


def draw_keys(key, part):
    key = jax.random.fold_in(key, 23)
    return scaled_field(key)


def draw_values(key, part):
    key = jax.random.fold_in(key, 37)
    sample = jnp.clip(jax.random.normal(key, (TOKENS, HEADS * HD), jnp.float32), -6.0, 6.0)
    return sample.astype(jnp.bfloat16)


def draw_windows(key, part):
    key = jax.random.fold_in(key, 41)
    key_one, key_two = jax.random.split(key)
    extents = (jax.random.randint(key_one, (HEADS, 3), 0, 4) > 0).astype(jnp.int32)
    shuffled = jax.random.permutation(key_two, HEADS)
    extents = extents.at[shuffled[0]].set(1)
    extents = extents.at[shuffled[1]].set(0)
    return extents


def setup_inputs(seed: int = 0) -> dict:
    key_of = jax.random.split(jax.random.key(seed), 7)
    queries = draw_queries(jax.random.fold_in(key_of[6], 71), 0)
    keys = draw_keys(jax.random.fold_in(key_of[6], 71), 0)
    values = draw_values(jax.random.fold_in(key_of[6], 71), 0)
    q_gain = jnp.clip(1.0 + 0.15 * jax.random.normal(key_of[3], (HD,), jnp.float32), 0.25, 1.75)
    k_gain = jnp.clip(1.0 + 0.15 * jax.random.normal(key_of[4], (HD,), jnp.float32), 0.25, 1.75)
    windows = draw_windows(jax.random.fold_in(key_of[6], 71), 0)
    return {"queries": queries, "keys": keys, "values": values, "q_gain": q_gain, "k_gain": k_gain, "windows": windows}


def normed(array, gain):
    widened = array.astype(jnp.float32)
    mean_sq = lax.optimization_barrier(jnp.mean(widened * widened, axis=-1, keepdims=True))
    return (widened * lax.rsqrt(mean_sq + 1e-06) * gain).astype(jnp.bfloat16)

def reference(queries, keys, values, q_gain, k_gain, windows):
    frames = SLAB_TF * N_SLAB
    score_scale = 1.0 / math.sqrt(HD)
    frame_index = jnp.arange(frames, dtype=jnp.int32)
    row_index = jnp.arange(GH, dtype=jnp.int32)
    column_index = jnp.arange(GW, dtype=jnp.int32)

    def one_head(head_index):

        def head_columns(array):
            return lax.dynamic_slice_in_dim(array, (head_index * HD).astype(jnp.int32), HD, 1)
        shape_tiles = (frames, GH, GW, TILE, HD)
        query_tiles = normed(head_columns(queries), q_gain).reshape(shape_tiles).astype(jnp.float32)
        key_tiles = normed(head_columns(keys), k_gain).reshape(shape_tiles)
        value_tiles = head_columns(values).reshape(shape_tiles)
        padded = jnp.pad(jnp.stack([key_tiles, value_tiles]), ((0, 0), (1, 1), (1, 1), (1, 1), (0, 0), (0, 0)))
        limits = windows[head_index]
        numerator = jnp.zeros(shape_tiles, jnp.float32)
        denominator = jnp.zeros(shape_tiles[:-1], jnp.float32)
        for shift_t in (-1, 0, 1):
            for shift_h in (-1, 0, 1):
                for shift_w in (-1, 0, 1):
                    key_part = padded[0, 1 + shift_t:1 + shift_t + frames, 1 + shift_h:1 + shift_h + GH, 1 + shift_w:1 + shift_w + GW]
                    value_part = padded[1, 1 + shift_t:1 + shift_t + frames, 1 + shift_h:1 + shift_h + GH, 1 + shift_w:1 + shift_w + GW]
                    scores = jnp.einsum('abcqd,abckd->abcqk', query_tiles, key_part.astype(jnp.float32)) * score_scale
                    inside_frame = (frame_index + shift_t >= 0) & (frame_index + shift_t < frames) & (abs(shift_t) <= limits[0])
                    inside_row = (row_index + shift_h >= 0) & (row_index + shift_h < GH) & (abs(shift_h) <= limits[1])
                    inside_column = (column_index + shift_w >= 0) & (column_index + shift_w < GW) & (abs(shift_w) <= limits[2])
                    inside = inside_frame[:, None, None] & inside_row[None, :, None] & inside_column[None, None, :]
                    weights = jnp.where(inside[..., None, None], jnp.exp(scores), jnp.float32(0.0))
                    denominator = denominator + lax.optimization_barrier(jnp.sum(weights, axis=-1))
                    numerator = numerator + jnp.einsum('abcqk,abckd->abcqd', weights.astype(jnp.bfloat16).astype(jnp.float32), value_part.astype(jnp.float32))
        return (numerator / denominator[..., None]).astype(jnp.bfloat16).reshape(TOKENS, HD)
    per_head = lax.map(one_head, jnp.arange(HEADS, dtype=jnp.int32))
    return jnp.transpose(per_head, (1, 0, 2)).reshape(TOKENS, HEADS * HD)
```

```python
import functools
import math

import jax
import jax.numpy as jnp
from jax import lax
from jax.experimental import pallas as pl
from jax.experimental.pallas import tpu as pltpu
from jax.sharding import PartitionSpec as P

TILE = 128
HEADS_PER_STEP = 4
VMEM_LIMIT = 48 * 2**20
F32 = jnp.float32
BF16 = jnp.bfloat16


def normed(block, gain):
    widened = block.astype(F32)
    mean_sq = jnp.mean(widened * widened, axis=-1, keepdims=True)
    return (widened * lax.rsqrt(mean_sq + 1e-06) * gain).astype(BF16)


def prep_kv_kernel(keys_ref, values_ref, gain_ref, out_ref):
    gain = gain_ref[...]
    for index in range(HEADS_PER_STEP):
        columns = slice(index * TILE, (index + 1) * TILE)
        out_ref[index, 0] = normed(keys_ref[:, columns], gain)
        out_ref[index, 1] = values_ref[:, columns]


def prep_q_kernel(queries_ref, gain_ref, out_ref):
    gain = gain_ref[...] * (math.log2(math.e) / math.sqrt(TILE))
    for index in range(HEADS_PER_STEP):
        columns = slice(index * TILE, (index + 1) * TILE)
        out_ref[index] = normed(queries_ref[:, columns], gain)


def merge_kernel(heads_ref, out_ref):
    for index in range(HEADS_PER_STEP):
        out_ref[:, index * TILE : (index + 1) * TILE] = heads_ref[index]


def prep_kv(keys, values, gain):
    steps = keys.shape[1] // (TILE * HEADS_PER_STEP)
    wide = pl.BlockSpec((TILE, TILE * HEADS_PER_STEP), lambda i: (0, i))
    return pl.pallas_call(
        prep_kv_kernel,
        grid=(steps,),
        in_specs=[wide, wide, pl.BlockSpec((1, TILE), lambda i: (0, 0))],
        out_specs=pl.BlockSpec((HEADS_PER_STEP, 2, TILE, TILE), lambda i: (i, 0, 0, 0)),
        out_shape=jax.ShapeDtypeStruct((steps * HEADS_PER_STEP, 2, TILE, TILE), BF16),
    )(keys, values, gain.reshape(1, TILE))


def prep_q(queries, gain):
    steps = queries.shape[1] // (TILE * HEADS_PER_STEP)
    return pl.pallas_call(
        prep_q_kernel,
        grid=(steps,),
        in_specs=[
            pl.BlockSpec((TILE, TILE * HEADS_PER_STEP), lambda i: (0, i)),
            pl.BlockSpec((1, TILE), lambda i: (0, 0)),
        ],
        out_specs=pl.BlockSpec((HEADS_PER_STEP, TILE, TILE), lambda i: (i, 0, 0)),
        out_shape=jax.ShapeDtypeStruct((steps * HEADS_PER_STEP, TILE, TILE), BF16),
    )(queries, gain.reshape(1, TILE))


def merge_heads(heads):
    steps = heads.shape[0] // HEADS_PER_STEP
    return pl.pallas_call(
        merge_kernel,
        grid=(steps,),
        in_specs=[pl.BlockSpec((HEADS_PER_STEP, TILE, TILE), lambda i: (i, 0, 0))],
        out_specs=pl.BlockSpec((TILE, TILE * HEADS_PER_STEP), lambda i: (0, i)),
        out_shape=jax.ShapeDtypeStruct((TILE, heads.shape[0] * TILE), BF16),
    )(heads)


def attend_kernel(
    slab_ref, windows_ref, q_ref, kv_ref, low_ref, high_ref, out_ref, sums, *, last_slab
):
    half_r, half_c = pl.program_id(0), pl.program_id(1)
    outer_r, inner_r, extra_r, first_r = 3 * half_r, 1 + half_r, 2 - half_r, 2 * half_r
    outer_c, inner_c, extra_c, first_c = 3 * half_c, 1 + half_c, 2 - half_c, 2 * half_c
    places = [(outer_r, outer_c), (outer_r, inner_c), (inner_r, outer_c), (inner_r, inner_c)]
    shared_r, shared_c = (first_r, first_r + 1), (first_c, first_c + 1)
    wide_t, wide_r, wide_c = (windows_ref[0, axis] >= 1 for axis in range(3))
    everything = wide_t & wide_r & wide_c
    has_low = slab_ref[0] > 0
    has_high = slab_ref[0] < last_slab
    groups = [
        ([0, 1, 2, 3], [(r, c) for r in shared_r for c in shared_c], None),
        ([1, 3], [(r, extra_c) for r in shared_r], wide_c),
        ([2, 3], [(extra_r, c) for c in shared_c], wide_r),
        ([3], [(extra_r, extra_c)], wide_r & wide_c),
    ]
    parts = [((1, 2), (0, 1), None), ((0,), (0,), has_low), ((3,), (1,), has_high)]

    def frame(index):
        if index == 0:
            return low_ref, 0
        if index == 3:
            return high_ref, 0
        return kv_ref, (index - 1) * 16

    def stack(blocks):
        return blocks[0] if len(blocks) == 1 else jnp.concatenate(blocks, axis=0)

    def bias(query, key):
        (place, t), (f, r, c) = query, key
        query_r, query_c = places[place]
        inside = wide_t if f - 1 != t else None
        for wide, a, b in ((wide_r, query_r, r), (wide_c, query_c, c)):
            near = wide | (a == b)
            inside = near if inside is None else inside & near
        return jnp.where(inside, 0.0, -1e30).astype(F32)

    def add(query_list, key_list, masked, first):
        q = stack([q_ref[(t * 4 + places[i][0]) * 4 + places[i][1]] for i, t in query_list])
        total = None
        for start in range(0, len(key_list), 2):
            chunk = key_list[start : start + 2]
            found = [(frame(f), r * 4 + c) for f, r, c in chunk]
            k = stack([ref[base + at, 0] for (ref, base), at in found])
            v = stack([ref[base + at, 1] for (ref, base), at in found])
            scores = lax.dot_general(q, k, (((1,), (1,)), ((), ())), preferred_element_type=F32)
            if masked:
                scores = scores + stack(
                    [
                        jnp.concatenate(
                            [jnp.full((TILE, TILE), bias(query, key)) for key in chunk], axis=1
                        )
                        for query in query_list
                    ]
                )
            weights = jnp.exp2(scores).astype(BF16)
            widened = jnp.concatenate([v, jnp.ones(v.shape, BF16)], axis=1)
            part = jnp.dot(weights, widened, preferred_element_type=F32)
            total = part if total is None else total + part
        for n, (i, t) in enumerate(query_list):
            rows = total[n * TILE : (n + 1) * TILE]
            if first:
                sums[i * 2 + t] = rows
            else:
                sums[i * 2 + t] += rows

    def run(masked):
        for frames, times, present in parts:
            for query_places, key_places, needed in groups:
                conditions = [] if present is None else [present]
                if masked:
                    conditions += [] if needed is None else [needed]
                    conditions += [wide_t] if present is not None else []
                queries = [(i, t) for i in query_places for t in times]
                keys = [(f, r, c) for f in frames for r, c in key_places]
                first = present is None and needed is None

                def all_queries(queries=queries, keys=keys, first=first):
                    for start in range(0, len(queries), 2):
                        add(queries[start : start + 2], keys, masked, first)

                if conditions:
                    pl.when(functools.reduce(lambda a, b: a & b, conditions))(all_queries)
                else:
                    all_queries()

    pl.when(everything)(lambda: run(False))
    pl.when(jnp.logical_not(everything))(lambda: run(True))
    for i, (r, c) in enumerate(places):
        for t in (0, 1):
            both = sums[i * 2 + t]
            out_ref[(t * 4 + r) * 4 + c] = (both[:, :TILE] / both[:, TILE:]).astype(BF16)


def attend(slab, last_slab, windows, q, kv, low, high):
    def whole(array):
        return pl.BlockSpec(array.shape, lambda i, j: (0,) * array.ndim)

    smem = pl.BlockSpec(memory_space=pltpu.SMEM)
    return pl.pallas_call(
        functools.partial(attend_kernel, last_slab=last_slab),
        grid=(2, 2),
        in_specs=[smem, smem] + [whole(x) for x in (q, kv, low, high)],
        out_specs=whole(q),
        out_shape=jax.ShapeDtypeStruct(q.shape, BF16),
        scratch_shapes=[pltpu.VMEM((8, TILE, 2 * TILE), F32)],
        compiler_params=pltpu.CompilerParams(vmem_limit_bytes=VMEM_LIMIT),
    )(slab, windows, q, kv, low, high)


def on_device(queries, keys, values, q_gain, k_gain, windows):
    slabs = lax.axis_size("slab")
    slab = lax.axis_index("slab").astype(jnp.int32).reshape(1)

    def exchange(array):
        return lax.all_to_all(array, "head", split_axis=0, concat_axis=0, tiled=True)

    kv = exchange(prep_kv(keys, values, k_gain))
    forward = [(i, i + 1) for i in range(slabs - 1)]
    backward = [(b, a) for a, b in forward]
    low = lax.ppermute(kv[16:], "slab", forward)
    high = lax.ppermute(kv[:16], "slab", backward)
    q = exchange(prep_q(queries, q_gain))
    result = attend(slab, slabs - 1, windows, q, kv, low, high)
    return merge_heads(exchange(result))


def solution(mesh):
    rows = P(("slab", "head"), None)
    return jax.shard_map(
        on_device,
        mesh=mesh,
        in_specs=(rows, rows, rows, P(), P(), P("head", None)),
        out_specs=rows,
        check_vma=False,
    )
```

```python
import functools
import math

import jax
import jax.numpy as jnp
from jax import lax
from jax.experimental import pallas as pl
from jax.experimental.pallas import tpu as pltpu
from jax.sharding import PartitionSpec as P

TILE = 128
ROWS = 4
FRAME = 16
PREP_HEADS = 16
PREP_VMEM = 60 * 2**20
SMALL_VMEM = 16 * 2**20
ATTEND_VMEM = 16 * 2**20
EXP2_SCALE = math.log2(math.e) / math.sqrt(TILE)
F32 = jnp.float32
BF16 = jnp.bfloat16
KEY, VALUE = 0, 1


def normed(block, gain):
    widened = block.astype(F32)
    mean_sq = jnp.mean(widened * widened, axis=-1, keepdims=True)
    return (widened * lax.rsqrt(mean_sq + 1e-06) * gain).astype(BF16)


def prep_kernel(queries_ref, keys_ref, values_ref, q_gain_ref, k_gain_ref, q_ref, kv_ref):
    q_gain, k_gain = q_gain_ref[...], k_gain_ref[...]
    for index in range(PREP_HEADS):
        columns = slice(index * TILE, (index + 1) * TILE)
        kv_ref[index, KEY] = normed(keys_ref[:, columns], k_gain)
        kv_ref[index, VALUE] = values_ref[:, columns]
        q_ref[index] = normed(queries_ref[:, columns], q_gain)


def prep(queries, keys, values, q_gain, k_gain):
    steps = keys.shape[1] // (TILE * PREP_HEADS)
    heads = steps * PREP_HEADS
    wide = pl.BlockSpec((TILE, TILE * PREP_HEADS), lambda i: (0, i))
    gain = pl.BlockSpec((1, TILE), lambda i: (0, 0))
    return pl.pallas_call(
        prep_kernel,
        grid=(steps,),
        in_specs=[wide, wide, wide, gain, gain],
        out_specs=[
            pl.BlockSpec((PREP_HEADS, TILE, TILE), lambda i: (i, 0, 0)),
            pl.BlockSpec((PREP_HEADS, 2, TILE, TILE), lambda i: (i, 0, 0, 0)),
        ],
        out_shape=[
            jax.ShapeDtypeStruct((heads, TILE, TILE), BF16),
            jax.ShapeDtypeStruct((heads, 2, TILE, TILE), BF16),
        ],
        compiler_params=pltpu.CompilerParams(vmem_limit_bytes=PREP_VMEM),
    )(queries, keys, values, q_gain.reshape(1, TILE), k_gain.reshape(1, TILE))


def merge_kernel(heads_ref, out_ref):
    for index in range(PREP_HEADS):
        out_ref[:, index * TILE : (index + 1) * TILE] = heads_ref[index]


def merge_heads(heads):
    steps = heads.shape[0] // PREP_HEADS
    return pl.pallas_call(
        merge_kernel,
        grid=(steps,),
        in_specs=[pl.BlockSpec((PREP_HEADS, TILE, TILE), lambda i: (i, 0, 0))],
        out_specs=pl.BlockSpec((TILE, TILE * PREP_HEADS), lambda i: (0, i)),
        out_shape=jax.ShapeDtypeStruct((TILE, heads.shape[0] * TILE), BF16),
        compiler_params=pltpu.CompilerParams(vmem_limit_bytes=SMALL_VMEM),
    )(heads)


def stack(blocks):
    return blocks[0] if len(blocks) == 1 else jnp.concatenate(blocks, axis=0)


def quarter(step, wide_r, wide_c):
    half_r, half_c = step // 2, step % 2
    outer_r, inner_r, extra_r, first_r = 3 * half_r, 1 + half_r, 2 - half_r, 2 * half_r
    outer_c, inner_c, extra_c, first_c = 3 * half_c, 1 + half_c, 2 - half_c, 2 * half_c
    places = [(outer_r, outer_c), (outer_r, inner_c), (inner_r, outer_c), (inner_r, inner_c)]
    shared_r, shared_c = (first_r, first_r + 1), (first_c, first_c + 1)
    groups = [
        ([0, 1, 2, 3], [(r, c) for r in shared_r for c in shared_c], None),
        ([1, 3], [(r, extra_c) for r in shared_r], wide_c),
        ([2, 3], [(extra_r, c) for c in shared_c], wide_r),
        ([3], [(extra_r, extra_c)], wide_r & wide_c),
    ]
    return places, groups


def weighted_sums(q, keys, values, ones, biases):
    total = None
    for start in range(0, len(keys), 2):
        k = stack(keys[start : start + 2])
        v = stack(values[start : start + 2])
        scores = lax.dot_general(q, k, (((1,), (1,)), ((), ())), preferred_element_type=F32)
        if biases is not None:
            scores = scores + stack(
                [
                    jnp.concatenate(
                        [jnp.full((TILE, TILE), b, F32) for b in row[start : start + 2]], axis=1
                    )
                    for row in biases
                ]
            )
        weights = jnp.exp2(scores * EXP2_SCALE).astype(BF16)
        widened = jnp.concatenate([v, jnp.full(v.shape, ones, BF16)], axis=1)
        part = jnp.dot(weights, widened, preferred_element_type=F32)
        total = part if total is None else total + part
    return total


def outside(conditions):
    inside = functools.reduce(lambda a, b: a & b, conditions)
    return jnp.where(inside, 0.0, -1e30).astype(F32)


def run_groups(groups, add):
    for query_places, key_places, needed in groups:
        action = functools.partial(add, query_places, key_places, needed is None)
        if needed is not None:
            pl.when(needed)(action)
        else:
            action()


def near_tiles(r, c):
    return [
        (a, b)
        for a in range(max(r - 1, 0), min(r + 2, ROWS))
        for b in range(max(c - 1, 0), min(c + 2, ROWS))
    ]


def own_kernel(windows_ref, q_ref, kv_ref, sums_ref):
    wide_t, wide_r, wide_c = (windows_ref[0, axis] >= 1 for axis in range(3))
    everything = wide_t & wide_r & wide_c

    def tile(t, place):
        return t * FRAME + place[0] * ROWS + place[1]

    def sums_of(place, keys, biases):
        return weighted_sums(
            stack([q_ref[tile(t, place)] for t in (0, 1)]),
            [kv_ref[tile(t, key), KEY] for t, key in keys],
            [kv_ref[tile(t, key), VALUE] for t, key in keys],
            1.0,
            biases,
        )

    def step(index, carry):
        places, groups = quarter(index, wide_r, wide_c)

        def add(query_places, key_places, first):
            keys = [(t, place) for t in (0, 1) for place in key_places]
            for i in query_places:
                r, c = places[i]
                biases = [
                    [
                        outside([wide_t | (t == u), wide_r | (r == kr), wide_c | (c == kc)])
                        for u, (kr, kc) in keys
                    ]
                    for t in (0, 1)
                ]
                total = sums_of(places[i], keys, biases)
                for t in (0, 1):
                    rows = total[t * TILE : (t + 1) * TILE]
                    at = tile(t, places[i])
                    if first:
                        sums_ref[at] = rows
                    else:
                        sums_ref[at] += rows

        run_groups(groups, add)
        return carry

    @pl.when(everything)
    def _():
        for r in range(ROWS):
            for c in range(ROWS):
                total = sums_of((r, c), [(t, key) for t in (0, 1) for key in near_tiles(r, c)], None)
                for t in (0, 1):
                    sums_ref[tile(t, (r, c))] = total[t * TILE : (t + 1) * TILE]

    @pl.when(jnp.logical_not(everything))
    def _():
        lax.fori_loop(0, 4, step, 0)


def halo_kernel(place_ref, windows_ref, q_ref, halo_ref, sums_ref, base_ref, out_ref, acc):
    del base_ref
    start = place_ref[0] * FRAME
    wide_t, wide_r, wide_c = (windows_ref[0, axis] >= 1 for axis in range(3))
    everything = wide_t & wide_r & wide_c
    ones = place_ref[1].astype(F32).astype(BF16)

    def finish(at, both):
        out_ref[at] = (both[:, :TILE] / both[:, TILE:]).astype(BF16)

    def sums_of(ats, key_places, biases):
        return weighted_sums(
            stack([q_ref[at] for at in ats]),
            [halo_ref[r * ROWS + c, KEY] for r, c in key_places],
            [halo_ref[r * ROWS + c, VALUE] for r, c in key_places],
            ones,
            biases,
        )

    def step(index, carry):
        places, groups = quarter(index, wide_r, wide_c)
        ats = [start + r * ROWS + c for r, c in places]
        for i in range(4):
            acc[i] = sums_ref[ats[i]]

        def add(query_places, key_places, first):
            for begin in range(0, len(query_places), 2):
                chosen = query_places[begin : begin + 2]
                biases = [
                    [
                        outside([wide_r | (places[i][0] == r), wide_c | (places[i][1] == c)])
                        for r, c in key_places
                    ]
                    for i in chosen
                ]
                total = sums_of([ats[i] for i in chosen], key_places, biases)
                for n, i in enumerate(chosen):
                    acc[i] += total[n * TILE : (n + 1) * TILE]

        run_groups(groups, add)
        for i in range(4):
            finish(ats[i], acc[i])
        return carry

    @pl.when(everything)
    def _():
        for r in range(ROWS):
            for c in range(ROWS):
                at = start + r * ROWS + c
                finish(at, sums_ref[at] + sums_of([at], near_tiles(r, c), None))

    @pl.when(wide_t & jnp.logical_not(everything))
    def _():
        lax.fori_loop(0, 4, step, 0)

    @pl.when(jnp.logical_not(wide_t))
    def _():
        for index in range(FRAME):
            finish(start + index, sums_ref[start + index])


SMEM_SPEC = pl.BlockSpec(memory_space=pltpu.SMEM)
VMEM_SPEC = pl.BlockSpec(memory_space=pltpu.VMEM)


def attend_own(windows, q, kv):
    return pl.pallas_call(
        own_kernel,
        in_specs=[SMEM_SPEC, VMEM_SPEC, VMEM_SPEC],
        out_specs=VMEM_SPEC,
        out_shape=jax.ShapeDtypeStruct((q.shape[0], TILE, 2 * TILE), F32),
        compiler_params=pltpu.CompilerParams(vmem_limit_bytes=ATTEND_VMEM),
        cost_estimate=pl.CostEstimate(
            flops=400 * 6 * TILE**3, bytes_accessed=2**23, transcendentals=400 * TILE**2
        ),
    )(windows, q, kv)


def attend_halo(place, windows, q, halo, sums, base):
    return pl.pallas_call(
        halo_kernel,
        in_specs=[SMEM_SPEC, SMEM_SPEC] + [VMEM_SPEC] * 4,
        out_specs=VMEM_SPEC,
        out_shape=jax.ShapeDtypeStruct(q.shape, BF16),
        input_output_aliases={5: 0},
        scratch_shapes=[pltpu.VMEM((4, TILE, 2 * TILE), F32)],
        compiler_params=pltpu.CompilerParams(vmem_limit_bytes=ATTEND_VMEM),
        cost_estimate=pl.CostEstimate(
            flops=100 * 6 * TILE**3, bytes_accessed=2**22, transcendentals=100 * TILE**2
        ),
    )(place, windows, q, halo, sums, base)


def on_device(queries, keys, values, q_gain, k_gain, windows):
    slabs = lax.axis_size("slab")
    slab = lax.axis_index("slab").astype(jnp.int32)
    odd = slab % 2

    def exchange(array):
        return lax.all_to_all(array, "head", split_axis=0, concat_axis=0, tiled=True)

    q, kv = prep(queries, keys, values, q_gain, k_gain)
    def together(kv):
        return exchange(kv)

    def apart(kv):
        return jnp.stack([exchange(kv[:, KEY]), exchange(kv[:, VALUE])], axis=1)

    kv = lax.cond(odd == 0, together, apart, kv)
    q = exchange(q)

    def frame_of(index):
        return lax.dynamic_slice(kv, (index * FRAME, 0, 0, 0), (FRAME, 2, TILE, TILE))

    def swap(block, low, high):
        pairs = [(a, a + 1) for a in range(low, high, 2)]
        return lax.ppermute(block, "slab", pairs + [(b, a) for a, b in pairs])

    far = swap(frame_of(odd), 1, slabs - 1)
    near = swap(frame_of(1 - odd), 0, slabs)
    far_present = ((slab > 0) & (slab < slabs - 1)).astype(jnp.int32)
    sums = attend_own(windows, q, kv)
    result = jnp.zeros(q.shape, BF16)
    result = attend_halo(jnp.stack([1 - odd, 1]), windows, q, near, sums, result)
    result = attend_halo(jnp.stack([odd, far_present]), windows, q, far, sums, result)
    return merge_heads(exchange(result))


def solution(mesh):
    rows = P(("slab", "head"), None)
    return jax.shard_map(
        on_device,
        mesh=mesh,
        in_specs=(rows, rows, rows, P(), P(), P("head", None)),
        out_specs=rows,
        check_vma=False,
    )
```

```python
import functools
import itertools
import math

import jax
import jax.numpy as jnp
from jax import lax
from jax.experimental import pallas as pl
from jax.experimental.pallas import tpu as pltpu
from jax.sharding import PartitionSpec as P

TILE = 128
ROWS = 4
FRAME = 16
PREP_HEADS = 16
PREP_VMEM = 60 * 2**20
SMALL_VMEM = 8 * 2**20
ATTEND_VMEM = 16 * 2**20
EXP2_SCALE = math.log2(math.e) / math.sqrt(TILE)
F32 = jnp.float32
BF16 = jnp.bfloat16
KEY, VALUE = 0, 1
ONE, BOTH = (TILE, TILE), (2, TILE, TILE)
SMEM_SPEC = pl.BlockSpec(memory_space=pltpu.SMEM)
VMEM_SPEC = pl.BlockSpec(memory_space=pltpu.VMEM)
ANY_SPEC = pl.BlockSpec(memory_space=pl.ANY)


def normed(block, gain):
    widened = block.astype(F32)
    mean_sq = jnp.mean(widened * widened, axis=-1, keepdims=True)
    return (widened * lax.rsqrt(mean_sq + 1e-06) * gain).astype(BF16)


def columns(index):
    return slice(index * TILE, (index + 1) * TILE)


def prep_kernel(queries_ref, keys_ref, values_ref, q_gain_ref, k_gain_ref, q_ref, kv_ref):
    q_gain, k_gain = q_gain_ref[...], k_gain_ref[...]
    for index in range(PREP_HEADS):
        block = columns(index)
        kv_ref[index, KEY] = normed(keys_ref[:, block], k_gain)
        kv_ref[index, VALUE] = values_ref[:, block]
        q_ref[index] = normed(queries_ref[:, block], q_gain)


def prep(queries, keys, values, q_gain, k_gain):
    steps = keys.shape[1] // (TILE * PREP_HEADS)
    heads = steps * PREP_HEADS
    wide = pl.BlockSpec((TILE, TILE * PREP_HEADS), lambda i: (0, i))
    gain = pl.BlockSpec((1, TILE), lambda i: (0, 0))
    return pl.pallas_call(
        prep_kernel,
        grid=(steps,),
        in_specs=[wide, wide, wide, gain, gain],
        out_specs=[
            pl.BlockSpec((PREP_HEADS, TILE, TILE), lambda i: (i, 0, 0)),
            pl.BlockSpec((PREP_HEADS, 2, TILE, TILE), lambda i: (i, 0, 0, 0)),
        ],
        out_shape=[
            jax.ShapeDtypeStruct((heads, TILE, TILE), BF16),
            jax.ShapeDtypeStruct((heads, 2, TILE, TILE), BF16),
        ],
        compiler_params=pltpu.CompilerParams(vmem_limit_bytes=PREP_VMEM),
    )(queries, keys, values, q_gain.reshape(1, TILE), k_gain.reshape(1, TILE))


def merge_kernel(heads_ref, out_ref):
    for index in range(PREP_HEADS):
        out_ref[:, columns(index)] = heads_ref[index]


def merge_heads(heads):
    steps = heads.shape[0] // PREP_HEADS
    return pl.pallas_call(
        merge_kernel,
        grid=(steps,),
        in_specs=[pl.BlockSpec((PREP_HEADS, TILE, TILE), lambda i: (i, 0, 0))],
        out_specs=pl.BlockSpec((TILE, TILE * PREP_HEADS), lambda i: (0, i)),
        out_shape=jax.ShapeDtypeStruct((TILE, heads.shape[0] * TILE), BF16),
        compiler_params=pltpu.CompilerParams(vmem_limit_bytes=SMALL_VMEM),
    )(heads)


def stack(blocks):
    return blocks[0] if len(blocks) == 1 else jnp.concatenate(blocks, axis=0)


def weighted_sums(q, keys, values, ones):
    total = None
    for start in range(0, len(keys), 2):
        k = stack(keys[start : start + 2])
        v = stack(values[start : start + 2])
        scores = lax.dot_general(q, k, (((1,), (1,)), ((), ())), preferred_element_type=F32)
        weights = jnp.exp2(scores * EXP2_SCALE).astype(BF16)
        widened = jnp.concatenate([v, jnp.full(v.shape, ones, BF16)], axis=1)
        part = jnp.dot(weights, widened, preferred_element_type=F32)
        total = part if total is None else total + part
    return total


def for_each_window(windows_ref, run):
    for wide in itertools.product((1, 0), repeat=windows_ref.shape[1]):
        same = [(windows_ref[0, axis] >= 1) == bool(w) for axis, w in enumerate(wide)]
        pl.when(functools.reduce(lambda x, y: x & y, same))(functools.partial(run, *wide))


def for_each_place(wide_r, wide_c, straight, visit):
    def near(r, c):
        return [
            a * ROWS + b
            for a in range(max(r - wide_r, 0), min(r + wide_r, ROWS - 1) + 1)
            for b in range(max(c - wide_c, 0), min(c + wide_c, ROWS - 1) + 1)
        ]

    if straight:
        for r, c in itertools.product(range(ROWS), repeat=2):
            visit(r * ROWS + c, near(r, c))
        return

    def reach(half, wide):
        outer, inner = 3 * half, 1 + half
        pair = [2 * half, 2 * half + 1]
        if wide:
            return [(outer, pair), (inner, pair + [2 - half])]
        return [(outer, [outer]), (inner, [inner])]

    def body(index, carry):
        for r, near_r in reach(index // 2, wide_r):
            for c, near_c in reach(index % 2, wide_c):
                visit(r * ROWS + c, [a * ROWS + b for a in near_r for b in near_c])
        return carry

    lax.fori_loop(0, 4, body, 0)


def own_kernel(windows_ref, q_ref, kv_ref, sums_ref):
    def run(wide_t, wide_r, wide_c):
        def visit(place, near_places):
            for times in ((0, 1),) if wide_t else ((0,), (1,)):
                ats = [t * FRAME + place for t in times]
                near = [t * FRAME + n for t in times for n in near_places]
                total = weighted_sums(
                    stack([q_ref[at] for at in ats]),
                    [kv_ref[at, KEY] for at in near],
                    [kv_ref[at, VALUE] for at in near],
                    1.0,
                )
                for n, at in enumerate(ats):
                    sums_ref[at] = total[n * TILE : (n + 1) * TILE]

        for_each_place(wide_r, wide_c, wide_t and wide_r and wide_c, visit)

    for_each_window(windows_ref, run)


def halo_kernel(place_ref, windows_ref, q_ref, near_ref, far_ref, sums_ref, out_ref):
    halos = (
        (near_ref, place_ref[0] * FRAME, 1.0),
        (far_ref, place_ref[1] * FRAME, place_ref[2].astype(F32).astype(BF16)),
    )

    def run(wide_t, wide_r, wide_c):
        def visit(place, near_places):
            for halo_ref, start, ones in halos:
                both = sums_ref[start + place]
                if wide_t:
                    both = both + weighted_sums(
                        q_ref[start + place],
                        [halo_ref[n, KEY] for n in near_places],
                        [halo_ref[n, VALUE] for n in near_places],
                        ones,
                    )
                out_ref[start + place] = (both[:, :TILE] / both[:, TILE:]).astype(BF16)

        for_each_place(wide_r, wide_c, wide_t and wide_r and wide_c, visit)

    for_each_window(windows_ref, run)


def attend_own(windows, q, kv):
    return pl.pallas_call(
        own_kernel,
        in_specs=[SMEM_SPEC] + [VMEM_SPEC] * 2,
        out_specs=VMEM_SPEC,
        out_shape=jax.ShapeDtypeStruct((q.shape[0], TILE, 2 * TILE), F32),
        compiler_params=pltpu.CompilerParams(vmem_limit_bytes=ATTEND_VMEM),
        cost_estimate=pl.CostEstimate(
            flops=400 * 6 * TILE**3, bytes_accessed=2**23, transcendentals=400 * TILE**2
        ),
    )(windows, q, kv)


def attend_halos(place, windows, q, near, far, sums):
    return pl.pallas_call(
        halo_kernel,
        in_specs=[SMEM_SPEC, SMEM_SPEC] + [VMEM_SPEC] * 4,
        out_specs=VMEM_SPEC,
        out_shape=jax.ShapeDtypeStruct(q.shape, BF16),
        compiler_params=pltpu.CompilerParams(vmem_limit_bytes=ATTEND_VMEM),
        cost_estimate=pl.CostEstimate(
            flops=200 * 6 * TILE**3, bytes_accessed=2**23, transcendentals=200 * TILE**2
        ),
    )(place, windows, q, near, far, sums)


def on_device(queries, keys, values, q_gain, k_gain, windows):
    slabs = lax.axis_size("slab")
    slab = lax.axis_index("slab").astype(jnp.int32)
    odd = slab % 2

    def exchange(array):
        return lax.all_to_all(array, "head", split_axis=0, concat_axis=0, tiled=True)

    def together(kv):
        return exchange(kv)

    def apart(kv):
        v = exchange(kv[:, VALUE])
        k = exchange(kv[:, KEY])
        return jnp.stack([k, v], axis=1)

    q, kv = prep(queries, keys, values, q_gain, k_gain)
    kv = lax.cond(odd == 0, together, apart, kv)
    q = exchange(q)

    def frame_of(index):
        return lax.dynamic_slice_in_dim(kv, index * FRAME, FRAME)

    def swap(block, low, high):
        pairs = [(a, a + 1) for a in range(low, high, 2)]
        return lax.ppermute(block, "slab", pairs + [(b, a) for a, b in pairs])

    far = swap(frame_of(odd), 1, slabs - 1)
    near = swap(frame_of(1 - odd), 0, slabs)
    far_present = ((slab > 0) & (slab < slabs - 1)).astype(jnp.int32)
    sums = attend_own(windows, q, kv)
    place = jnp.stack([1 - odd, odd, far_present])
    return merge_heads(exchange(attend_halos(place, windows, q, near, far, sums)))


def solution(mesh):
    rows = P(("slab", "head"), None)
    return jax.shard_map(
        on_device,
        mesh=mesh,
        in_specs=(rows, rows, rows, P(), P(), P("head", None)),
        out_specs=rows,
        check_vma=False,
    )
```

```python
import functools
import itertools
import math

import jax
import jax.numpy as jnp
from jax import lax
from jax.experimental import pallas as pl
from jax.experimental.pallas import tpu as pltpu
from jax.sharding import PartitionSpec as P

TILE = 128
ROWS = 4
FRAME = 16
PREP_HEADS = 16
PREP_VMEM = 60 * 2**20
SMALL_VMEM = 8 * 2**20
ATTEND_VMEM = 16 * 2**20
NEAR_COST = pl.CostEstimate(flops=0, bytes_accessed=0, transcendentals=0)
FAR_COST = pl.CostEstimate(
    flops=600 * TILE**3, bytes_accessed=2**22, transcendentals=100 * TILE**2
)
EXP2_SCALE = math.log2(math.e) / math.sqrt(TILE)
F32 = jnp.float32
BF16 = jnp.bfloat16
KEY, VALUE = 0, 1
ONE, BOTH = (TILE, TILE), (2, TILE, TILE)
SMEM_SPEC = pl.BlockSpec(memory_space=pltpu.SMEM)
VMEM_SPEC = pl.BlockSpec(memory_space=pltpu.VMEM)
ANY_SPEC = pl.BlockSpec(memory_space=pl.ANY)


def normed(block, gain):
    widened = block.astype(F32)
    mean_sq = jnp.mean(widened * widened, axis=-1, keepdims=True)
    return (widened * lax.rsqrt(mean_sq + 1e-06) * gain).astype(BF16)


def columns(index):
    return slice(index * TILE, (index + 1) * TILE)


def prep_kernel(queries_ref, keys_ref, values_ref, q_gain_ref, k_gain_ref, q_ref, kv_ref):
    q_gain, k_gain = q_gain_ref[...], k_gain_ref[...]
    for index in range(PREP_HEADS):
        block = columns(index)
        kv_ref[index, KEY] = normed(keys_ref[:, block], k_gain)
        kv_ref[index, VALUE] = values_ref[:, block]
        q_ref[index] = normed(queries_ref[:, block], q_gain)


def prep(queries, keys, values, q_gain, k_gain):
    steps = keys.shape[1] // (TILE * PREP_HEADS)
    heads = steps * PREP_HEADS
    wide = pl.BlockSpec((TILE, TILE * PREP_HEADS), lambda i: (0, i))
    gain = pl.BlockSpec((1, TILE), lambda i: (0, 0))
    return pl.pallas_call(
        prep_kernel,
        grid=(steps,),
        in_specs=[wide, wide, wide, gain, gain],
        out_specs=[
            pl.BlockSpec((PREP_HEADS, TILE, TILE), lambda i: (i, 0, 0)),
            pl.BlockSpec((PREP_HEADS, 2, TILE, TILE), lambda i: (i, 0, 0, 0)),
        ],
        out_shape=[
            jax.ShapeDtypeStruct((heads, TILE, TILE), BF16),
            jax.ShapeDtypeStruct((heads, 2, TILE, TILE), BF16),
        ],
        compiler_params=pltpu.CompilerParams(vmem_limit_bytes=PREP_VMEM),
    )(queries, keys, values, q_gain.reshape(1, TILE), k_gain.reshape(1, TILE))


def merge_kernel(heads_ref, out_ref):
    for index in range(PREP_HEADS):
        out_ref[:, columns(index)] = heads_ref[index]


def merge_heads(heads):
    steps = heads.shape[0] // PREP_HEADS
    return pl.pallas_call(
        merge_kernel,
        grid=(steps,),
        in_specs=[pl.BlockSpec((PREP_HEADS, TILE, TILE), lambda i: (i, 0, 0))],
        out_specs=pl.BlockSpec((TILE, TILE * PREP_HEADS), lambda i: (0, i)),
        out_shape=jax.ShapeDtypeStruct((TILE, heads.shape[0] * TILE), BF16),
        compiler_params=pltpu.CompilerParams(vmem_limit_bytes=SMALL_VMEM),
    )(heads)


def stack(blocks):
    return blocks[0] if len(blocks) == 1 else jnp.concatenate(blocks, axis=0)


def weighted_sums(q, keys, values, ones):
    total = None
    for start in range(0, len(keys), 2):
        k = stack(keys[start : start + 2])
        v = stack(values[start : start + 2])
        scores = lax.dot_general(q, k, (((1,), (1,)), ((), ())), preferred_element_type=F32)
        weights = jnp.exp2(scores * EXP2_SCALE).astype(BF16)
        widened = jnp.concatenate([v, jnp.full(v.shape, ones, BF16)], axis=1)
        part = jnp.dot(weights, widened, preferred_element_type=F32)
        total = part if total is None else total + part
    return total


def for_each_window(windows_ref, run):
    for wide in itertools.product((1, 0), repeat=windows_ref.shape[1]):
        same = [(windows_ref[0, axis] >= 1) == bool(w) for axis, w in enumerate(wide)]
        pl.when(functools.reduce(lambda x, y: x & y, same))(functools.partial(run, *wide))


def for_each_place(wide_r, wide_c, straight, visit):
    def near(r, c):
        return [
            a * ROWS + b
            for a in range(max(r - wide_r, 0), min(r + wide_r, ROWS - 1) + 1)
            for b in range(max(c - wide_c, 0), min(c + wide_c, ROWS - 1) + 1)
        ]

    if straight:
        for r, c in itertools.product(range(ROWS), repeat=2):
            visit(r * ROWS + c, near(r, c))
        return

    def reach(half, wide):
        outer, inner = 3 * half, 1 + half
        pair = [2 * half, 2 * half + 1]
        if wide:
            return [(outer, pair), (inner, pair + [2 - half])]
        return [(outer, [outer]), (inner, [inner])]

    def body(index, carry):
        for r, near_r in reach(index // 2, wide_r):
            for c, near_c in reach(index % 2, wide_c):
                visit(r * ROWS + c, [a * ROWS + b for a in near_r for b in near_c])
        return carry

    lax.fori_loop(0, 4, body, 0)


def own_kernel(windows_ref, q_ref, kv_ref, sums_ref):
    def run(wide_t, wide_r, wide_c):
        def visit(place, near_places):
            for times in ((0, 1),) if wide_t else ((0,), (1,)):
                ats = [t * FRAME + place for t in times]
                near = [t * FRAME + n for t in times for n in near_places]
                total = weighted_sums(
                    stack([q_ref[at] for at in ats]),
                    [kv_ref[at, KEY] for at in near],
                    [kv_ref[at, VALUE] for at in near],
                    1.0,
                )
                for n, at in enumerate(ats):
                    sums_ref[at] = total[n * TILE : (n + 1) * TILE]

        for_each_place(wide_r, wide_c, wide_t and wide_r and wide_c, visit)

    for_each_window(windows_ref, run)


def halo_kernel(place_ref, windows_ref, q_ref, halo_ref, sums_ref, base_ref, out_ref):
    del base_ref
    start = place_ref[0] * FRAME
    ones = place_ref[1].astype(F32).astype(BF16)

    def run(wide_t, wide_r, wide_c):
        def visit(place, near_places):
            both = sums_ref[start + place]
            if wide_t:
                both = both + weighted_sums(
                    q_ref[start + place],
                    [halo_ref[n, KEY] for n in near_places],
                    [halo_ref[n, VALUE] for n in near_places],
                    ones,
                )
            out_ref[start + place] = (both[:, :TILE] / both[:, TILE:]).astype(BF16)

        for_each_place(wide_r, wide_c, wide_t and wide_r and wide_c, visit)

    for_each_window(windows_ref, run)


def attend_own(windows, q, kv):
    return pl.pallas_call(
        own_kernel,
        in_specs=[SMEM_SPEC] + [VMEM_SPEC] * 2,
        out_specs=VMEM_SPEC,
        out_shape=jax.ShapeDtypeStruct((q.shape[0], TILE, 2 * TILE), F32),
        compiler_params=pltpu.CompilerParams(vmem_limit_bytes=ATTEND_VMEM),
        cost_estimate=pl.CostEstimate(
            flops=400 * 6 * TILE**3, bytes_accessed=2**23, transcendentals=400 * TILE**2
        ),
    )(windows, q, kv)


def attend_halo(place, windows, q, halo, sums, base, cost):
    return pl.pallas_call(
        halo_kernel,
        in_specs=[SMEM_SPEC, SMEM_SPEC] + [VMEM_SPEC] * 4,
        out_specs=VMEM_SPEC,
        out_shape=jax.ShapeDtypeStruct(q.shape, BF16),
        input_output_aliases={5: 0},
        compiler_params=pltpu.CompilerParams(vmem_limit_bytes=ATTEND_VMEM),
        cost_estimate=cost,
    )(place, windows, q, halo, sums, base)


def on_device(queries, keys, values, q_gain, k_gain, windows):
    slabs = lax.axis_size("slab")
    slab = lax.axis_index("slab").astype(jnp.int32)
    odd = slab % 2

    def exchange(array):
        return lax.all_to_all(array, "head", split_axis=0, concat_axis=0, tiled=True)

    def together(kv):
        return exchange(kv)

    def apart(kv):
        v = exchange(kv[:, VALUE])
        k = exchange(kv[:, KEY])
        return jnp.stack([k, v], axis=1)

    q, kv = prep(queries, keys, values, q_gain, k_gain)
    kv = lax.cond(odd == 0, together, apart, kv)
    q = exchange(q)

    def frame_of(index):
        return lax.dynamic_slice_in_dim(kv, index * FRAME, FRAME)

    def swap(block, low, high):
        pairs = [(a, a + 1) for a in range(low, high, 2)]
        return lax.ppermute(block, "slab", pairs + [(b, a) for a, b in pairs])

    far = swap(frame_of(odd), 1, slabs - 1)
    near = swap(frame_of(1 - odd), 0, slabs)
    far_present = ((slab > 0) & (slab < slabs - 1)).astype(jnp.int32)
    sums = attend_own(windows, q, kv)
    result = jnp.zeros(q.shape, BF16)
    result = attend_halo(jnp.stack([1 - odd, 1]), windows, q, near, sums, result, NEAR_COST)
    result = attend_halo(jnp.stack([odd, far_present]), windows, q, far, sums, result, FAR_COST)
    return merge_heads(exchange(result))


def solution(mesh):
    rows = P(("slab", "head"), None)
    return jax.shard_map(
        on_device,
        mesh=mesh,
        in_specs=(rows, rows, rows, P(), P(), P("head", None)),
        out_specs=rows,
        check_vma=False,
    )
```

```python
import functools
import itertools
import math

import jax
import jax.numpy as jnp
from jax import lax
from jax.experimental import pallas as pl
from jax.experimental.pallas import tpu as pltpu
from jax.sharding import PartitionSpec as P

TILE = 128
ROWS = 4
FRAME = 16
PREP_HEADS = 16
PREP_VMEM = 60 * 2**20
SMALL_VMEM = 8 * 2**20
ATTEND_VMEM = 16 * 2**20
NEAR_COST = pl.CostEstimate(flops=0, bytes_accessed=0, transcendentals=0)
FAR_COST = pl.CostEstimate(
    flops=600 * TILE**3, bytes_accessed=2**22, transcendentals=100 * TILE**2
)
EXP2_SCALE = math.log2(math.e) / math.sqrt(TILE)
F32 = jnp.float32
BF16 = jnp.bfloat16
KEY, VALUE = 0, 1
ONE, BOTH = (TILE, TILE), (2, TILE, TILE)
SMEM_SPEC = pl.BlockSpec(memory_space=pltpu.SMEM)
VMEM_SPEC = pl.BlockSpec(memory_space=pltpu.VMEM)
ANY_SPEC = pl.BlockSpec(memory_space=pl.ANY)


def normed(block, gain):
    widened = block.astype(F32)
    mean_sq = jnp.mean(widened * widened, axis=-1, keepdims=True)
    return (widened * lax.rsqrt(mean_sq + 1e-06) * gain).astype(BF16)


def columns(index):
    return slice(index * TILE, (index + 1) * TILE)


def prep_kernel(queries_ref, keys_ref, values_ref, q_gain_ref, k_gain_ref, q_ref, kv_ref):
    q_gain, k_gain = q_gain_ref[...], k_gain_ref[...]
    for index in range(PREP_HEADS):
        block = columns(index)
        kv_ref[index, KEY] = normed(keys_ref[:, block], k_gain)
        kv_ref[index, VALUE] = values_ref[:, block]
        q_ref[index] = normed(queries_ref[:, block], q_gain)


def prep(queries, keys, values, q_gain, k_gain):
    steps = keys.shape[1] // (TILE * PREP_HEADS)
    heads = steps * PREP_HEADS
    wide = pl.BlockSpec((TILE, TILE * PREP_HEADS), lambda i: (0, i))
    gain = pl.BlockSpec((1, TILE), lambda i: (0, 0))
    return pl.pallas_call(
        prep_kernel,
        grid=(steps,),
        in_specs=[wide, wide, wide, gain, gain],
        out_specs=[
            pl.BlockSpec((PREP_HEADS, TILE, TILE), lambda i: (i, 0, 0)),
            pl.BlockSpec((PREP_HEADS, 2, TILE, TILE), lambda i: (i, 0, 0, 0)),
        ],
        out_shape=[
            jax.ShapeDtypeStruct((heads, TILE, TILE), BF16),
            jax.ShapeDtypeStruct((heads, 2, TILE, TILE), BF16),
        ],
        compiler_params=pltpu.CompilerParams(vmem_limit_bytes=PREP_VMEM),
    )(queries, keys, values, q_gain.reshape(1, TILE), k_gain.reshape(1, TILE))


def merge_kernel(heads_ref, out_ref):
    for index in range(PREP_HEADS):
        out_ref[:, columns(index)] = heads_ref[index]


def merge_heads(heads):
    steps = heads.shape[0] // PREP_HEADS
    return pl.pallas_call(
        merge_kernel,
        grid=(steps,),
        in_specs=[pl.BlockSpec((PREP_HEADS, TILE, TILE), lambda i: (i, 0, 0))],
        out_specs=pl.BlockSpec((TILE, TILE * PREP_HEADS), lambda i: (0, i)),
        out_shape=jax.ShapeDtypeStruct((TILE, heads.shape[0] * TILE), BF16),
        compiler_params=pltpu.CompilerParams(vmem_limit_bytes=SMALL_VMEM),
    )(heads)


def stack(blocks):
    return blocks[0] if len(blocks) == 1 else jnp.concatenate(blocks, axis=0)


def weighted_sums(q, keys, values, ones):
    total = None
    for start in range(0, len(keys), 2):
        k = stack(keys[start : start + 2])
        v = stack(values[start : start + 2])
        scores = lax.dot_general(q, k, (((1,), (1,)), ((), ())), preferred_element_type=F32)
        weights = jnp.exp2(scores * EXP2_SCALE).astype(BF16)
        widened = jnp.concatenate([v, jnp.full(v.shape, ones, BF16)], axis=1)
        part = jnp.dot(weights, widened, preferred_element_type=F32)
        total = part if total is None else total + part
    return total


def for_each_window(windows_ref, run):
    for wide in itertools.product((1, 0), repeat=windows_ref.shape[1]):
        same = [(windows_ref[0, axis] >= 1) == bool(w) for axis, w in enumerate(wide)]
        pl.when(functools.reduce(lambda x, y: x & y, same))(functools.partial(run, *wide))


def for_each_place(wide_r, wide_c, straight, visit):
    def near(r, c):
        return [
            a * ROWS + b
            for a in range(max(r - wide_r, 0), min(r + wide_r, ROWS - 1) + 1)
            for b in range(max(c - wide_c, 0), min(c + wide_c, ROWS - 1) + 1)
        ]

    if straight:
        for r, c in itertools.product(range(ROWS), repeat=2):
            visit(r * ROWS + c, near(r, c))
        return

    def reach(half, wide):
        outer, inner = 3 * half, 1 + half
        pair = [2 * half, 2 * half + 1]
        if wide:
            return [(outer, pair), (inner, pair + [2 - half])]
        return [(outer, [outer]), (inner, [inner])]

    def body(index, carry):
        for r, near_r in reach(index // 2, wide_r):
            for c, near_c in reach(index % 2, wide_c):
                visit(r * ROWS + c, [a * ROWS + b for a in near_r for b in near_c])
        return carry

    lax.fori_loop(0, 4, body, 0)


def own_kernel(windows_ref, q_ref, kv_ref, sums_ref):
    def run(wide_t, wide_r, wide_c):
        def visit(place, near_places):
            for times in ((0, 1),) if wide_t else ((0,), (1,)):
                ats = [t * FRAME + place for t in times]
                near = [t * FRAME + n for t in times for n in near_places]
                total = weighted_sums(
                    stack([q_ref[at] for at in ats]),
                    [kv_ref[at, KEY] for at in near],
                    [kv_ref[at, VALUE] for at in near],
                    1.0,
                )
                for n, at in enumerate(ats):
                    sums_ref[at] = total[n * TILE : (n + 1) * TILE]

        for_each_place(wide_r, wide_c, wide_t and wide_r and wide_c, visit)

    for_each_window(windows_ref, run)


def halo_kernel(place_ref, windows_ref, q_ref, halo_ref, sums_ref, *results):
    out_ref = results[-1]
    for base_ref in results[:-1]:
        other = FRAME - place_ref[0] * FRAME
        out_ref[pl.ds(other, FRAME)] = base_ref[pl.ds(other, FRAME)]
    start = place_ref[0] * FRAME
    ones = place_ref[1].astype(F32).astype(BF16)

    def run(wide_t, wide_r, wide_c):
        def visit(place, near_places):
            both = sums_ref[start + place]
            if wide_t:
                both = both + weighted_sums(
                    q_ref[start + place],
                    [halo_ref[n, KEY] for n in near_places],
                    [halo_ref[n, VALUE] for n in near_places],
                    ones,
                )
            out_ref[start + place] = (both[:, :TILE] / both[:, TILE:]).astype(BF16)

        for_each_place(wide_r, wide_c, wide_t and wide_r and wide_c, visit)

    for_each_window(windows_ref, run)


def attend_own(windows, q, kv):
    return pl.pallas_call(
        own_kernel,
        in_specs=[SMEM_SPEC] + [VMEM_SPEC] * 2,
        out_specs=VMEM_SPEC,
        out_shape=jax.ShapeDtypeStruct((q.shape[0], TILE, 2 * TILE), F32),
        compiler_params=pltpu.CompilerParams(vmem_limit_bytes=ATTEND_VMEM),
        cost_estimate=pl.CostEstimate(
            flops=400 * 6 * TILE**3, bytes_accessed=2**23, transcendentals=400 * TILE**2
        ),
    )(windows, q, kv)


def attend_halo(place, windows, q, halo, sums, cost, base=()):
    return pl.pallas_call(
        halo_kernel,
        in_specs=[SMEM_SPEC, SMEM_SPEC] + [VMEM_SPEC] * (3 + len(base)),
        out_specs=VMEM_SPEC,
        out_shape=jax.ShapeDtypeStruct(q.shape, BF16),
        compiler_params=pltpu.CompilerParams(vmem_limit_bytes=ATTEND_VMEM),
        cost_estimate=cost,
    )(place, windows, q, halo, sums, *base)


def on_device(queries, keys, values, q_gain, k_gain, windows):
    slabs = lax.axis_size("slab")
    slab = lax.axis_index("slab").astype(jnp.int32)
    odd = slab % 2

    def exchange(array):
        return lax.all_to_all(array, "head", split_axis=0, concat_axis=0, tiled=True)

    def together(kv):
        return exchange(kv)

    def apart(kv):
        v = exchange(kv[:, VALUE])
        k = exchange(kv[:, KEY])
        return jnp.stack([k, v], axis=1)

    q, kv = prep(queries, keys, values, q_gain, k_gain)
    kv = lax.cond(odd == 0, together, apart, kv)
    q = exchange(q)

    def frame_of(index):
        return lax.dynamic_slice_in_dim(kv, index * FRAME, FRAME)

    def swap(block, low, high):
        pairs = [(a, a + 1) for a in range(low, high, 2)]
        return lax.ppermute(block, "slab", pairs + [(b, a) for a, b in pairs])

    far = swap(frame_of(odd), 1, slabs - 1)
    near = swap(frame_of(1 - odd), 0, slabs)
    far_present = ((slab > 0) & (slab < slabs - 1)).astype(jnp.int32)
    sums = attend_own(windows, q, kv)
    result = attend_halo(jnp.stack([1 - odd, 1]), windows, q, near, sums, NEAR_COST)
    result = attend_halo(jnp.stack([odd, far_present]), windows, q, far, sums, FAR_COST, (result,))
    return merge_heads(exchange(result))


def solution(mesh):
    rows = P(("slab", "head"), None)
    return jax.shard_map(
        on_device,
        mesh=mesh,
        in_specs=(rows, rows, rows, P(), P(), P("head", None)),
        out_specs=rows,
        check_vma=False,
    )
```

```python
import functools
import itertools
import math

import jax
import jax.numpy as jnp
from jax import lax
from jax.experimental import pallas as pl
from jax.experimental.pallas import tpu as pltpu
from jax.sharding import PartitionSpec as P

TILE = 128
ROWS = 4
FRAME = 16
PREP_HEADS = 16
PREP_VMEM = 60 * 2**20
SMALL_VMEM = 8 * 2**20
ATTEND_VMEM = 16 * 2**20
NEAR_COST = pl.CostEstimate(flops=0, bytes_accessed=0, transcendentals=0)
FAR_COST = pl.CostEstimate(
    flops=600 * TILE**3, bytes_accessed=2**22, transcendentals=100 * TILE**2
)
EXP2_SCALE = math.log2(math.e) / math.sqrt(TILE)
F32 = jnp.float32
BF16 = jnp.bfloat16
KEY, VALUE = 0, 1
ONE, BOTH = (TILE, TILE), (2, TILE, TILE)
SMEM_SPEC = pl.BlockSpec(memory_space=pltpu.SMEM)
VMEM_SPEC = pl.BlockSpec(memory_space=pltpu.VMEM)
ANY_SPEC = pl.BlockSpec(memory_space=pl.ANY)


def normed(block, gain):
    widened = block.astype(F32)
    mean_sq = jnp.mean(widened * widened, axis=-1, keepdims=True)
    return (widened * lax.rsqrt(mean_sq + 1e-06) * gain).astype(BF16)


def columns(index):
    return slice(index * TILE, (index + 1) * TILE)


def prep_kernel(queries_ref, keys_ref, values_ref, q_gain_ref, k_gain_ref, q_ref, kv_ref):
    q_gain, k_gain = q_gain_ref[...], k_gain_ref[...]
    for index in range(PREP_HEADS):
        block = columns(index)
        kv_ref[index, KEY] = normed(keys_ref[:, block], k_gain)
        kv_ref[index, VALUE] = values_ref[:, block]
        q_ref[index] = normed(queries_ref[:, block], q_gain)


def prep(queries, keys, values, q_gain, k_gain):
    steps = keys.shape[1] // (TILE * PREP_HEADS)
    heads = steps * PREP_HEADS
    wide = pl.BlockSpec((TILE, TILE * PREP_HEADS), lambda i: (0, i))
    gain = pl.BlockSpec((1, TILE), lambda i: (0, 0))
    return pl.pallas_call(
        prep_kernel,
        grid=(steps,),
        in_specs=[wide, wide, wide, gain, gain],
        out_specs=[
            pl.BlockSpec((PREP_HEADS, TILE, TILE), lambda i: (i, 0, 0)),
            pl.BlockSpec((PREP_HEADS, 2, TILE, TILE), lambda i: (i, 0, 0, 0)),
        ],
        out_shape=[
            jax.ShapeDtypeStruct((heads, TILE, TILE), BF16),
            jax.ShapeDtypeStruct((heads, 2, TILE, TILE), BF16),
        ],
        compiler_params=pltpu.CompilerParams(vmem_limit_bytes=PREP_VMEM),
    )(queries, keys, values, q_gain.reshape(1, TILE), k_gain.reshape(1, TILE))


def merge_kernel(heads_ref, out_ref):
    for index in range(PREP_HEADS):
        out_ref[:, columns(index)] = heads_ref[index]


def merge_heads(heads):
    steps = heads.shape[0] // PREP_HEADS
    return pl.pallas_call(
        merge_kernel,
        grid=(steps,),
        in_specs=[pl.BlockSpec((PREP_HEADS, TILE, TILE), lambda i: (i, 0, 0))],
        out_specs=pl.BlockSpec((TILE, TILE * PREP_HEADS), lambda i: (0, i)),
        out_shape=jax.ShapeDtypeStruct((TILE, heads.shape[0] * TILE), BF16),
        compiler_params=pltpu.CompilerParams(vmem_limit_bytes=SMALL_VMEM),
    )(heads)


def stack(blocks):
    return blocks[0] if len(blocks) == 1 else jnp.concatenate(blocks, axis=0)


def weighted_sums(q, keys, values, ones):
    total = None
    for start in range(0, len(keys), 2):
        k = stack(keys[start : start + 2])
        v = stack(values[start : start + 2])
        scores = lax.dot_general(q, k, (((1,), (1,)), ((), ())), preferred_element_type=F32)
        weights = jnp.exp2(scores * EXP2_SCALE).astype(BF16)
        widened = jnp.concatenate([v, jnp.full(v.shape, ones, BF16)], axis=1)
        part = jnp.dot(weights, widened, preferred_element_type=F32)
        total = part if total is None else total + part
    return total


def for_each_window(windows_ref, run):
    for wide in itertools.product((1, 0), repeat=windows_ref.shape[1]):
        same = [(windows_ref[0, axis] >= 1) == bool(w) for axis, w in enumerate(wide)]
        pl.when(functools.reduce(lambda x, y: x & y, same))(functools.partial(run, *wide))


def for_each_place(wide_r, wide_c, straight, visit):
    def near(r, c):
        return [
            a * ROWS + b
            for a in range(max(r - wide_r, 0), min(r + wide_r, ROWS - 1) + 1)
            for b in range(max(c - wide_c, 0), min(c + wide_c, ROWS - 1) + 1)
        ]

    if straight:
        for r, c in itertools.product(range(ROWS), repeat=2):
            visit(r * ROWS + c, near(r, c))
        return

    def reach(half, wide):
        outer, inner = 3 * half, 1 + half
        pair = [2 * half, 2 * half + 1]
        if wide:
            return [(outer, pair), (inner, pair + [2 - half])]
        return [(outer, [outer]), (inner, [inner])]

    def body(index, carry):
        for r, near_r in reach(index // 2, wide_r):
            for c, near_c in reach(index % 2, wide_c):
                visit(r * ROWS + c, [a * ROWS + b for a in near_r for b in near_c])
        return carry

    lax.fori_loop(0, 4, body, 0)


def own_kernel(windows_ref, q_ref, kv_ref, sums_ref):
    def run(wide_t, wide_r, wide_c):
        def visit(place, near_places):
            for times in ((0, 1),) if wide_t else ((0,), (1,)):
                ats = [t * FRAME + place for t in times]
                near = [t * FRAME + n for t in times for n in near_places]
                total = weighted_sums(
                    stack([q_ref[at] for at in ats]),
                    [kv_ref[at, KEY] for at in near],
                    [kv_ref[at, VALUE] for at in near],
                    1.0,
                )
                for n, at in enumerate(ats):
                    sums_ref[at] = total[n * TILE : (n + 1) * TILE]

        for_each_place(wide_r, wide_c, wide_t and wide_r and wide_c, visit)

    for_each_window(windows_ref, run)


def halo_kernel(place_ref, windows_ref, q_ref, halo_ref, sums_ref, *results):
    out_ref = results[-1]
    for base_ref in results[:-1]:
        other = FRAME - place_ref[0] * FRAME
        out_ref[pl.ds(other, FRAME)] = base_ref[pl.ds(other, FRAME)]
    start = place_ref[0] * FRAME
    ones = place_ref[1].astype(F32).astype(BF16)

    def run(wide_t, wide_r, wide_c):
        def visit(place, near_places):
            both = sums_ref[start + place]
            if wide_t:
                both = both + weighted_sums(
                    q_ref[start + place],
                    [halo_ref[n, KEY] for n in near_places],
                    [halo_ref[n, VALUE] for n in near_places],
                    ones,
                )
            out_ref[start + place] = (both[:, :TILE] / both[:, TILE:]).astype(BF16)

        for_each_place(wide_r, wide_c, wide_t and wide_r and wide_c, visit)

    for_each_window(windows_ref, run)


def attend_own(windows, q, kv):
    return pl.pallas_call(
        own_kernel,
        in_specs=[SMEM_SPEC] + [VMEM_SPEC] * 2,
        out_specs=VMEM_SPEC,
        out_shape=jax.ShapeDtypeStruct((q.shape[0], TILE, 2 * TILE), F32),
        compiler_params=pltpu.CompilerParams(vmem_limit_bytes=ATTEND_VMEM),
        cost_estimate=pl.CostEstimate(
            flops=400 * 6 * TILE**3, bytes_accessed=2**23, transcendentals=400 * TILE**2
        ),
    )(windows, q, kv)


def attend_halo(place, windows, q, halo, sums, cost, base=()):
    return pl.pallas_call(
        halo_kernel,
        in_specs=[SMEM_SPEC, SMEM_SPEC] + [VMEM_SPEC] * (3 + len(base)),
        out_specs=VMEM_SPEC,
        out_shape=jax.ShapeDtypeStruct(q.shape, BF16),
        compiler_params=pltpu.CompilerParams(vmem_limit_bytes=ATTEND_VMEM),
        cost_estimate=cost,
    )(place, windows, q, halo, sums, *base)


def on_device(queries, keys, values, q_gain, k_gain, windows):
    slabs = lax.axis_size("slab")
    slab = lax.axis_index("slab").astype(jnp.int32)
    odd = slab % 2

    def exchange(array):
        return lax.all_to_all(array, "head", split_axis=0, concat_axis=0, tiled=True)

    def together(kv):
        return exchange(kv)

    def apart(kv):
        v, rest = lax.optimization_barrier((kv[:, VALUE], kv))
        v = exchange(v)
        k = exchange(rest[:, KEY])
        return jnp.stack([k, v], axis=1)

    q, kv = prep(queries, keys, values, q_gain, k_gain)
    kv = lax.cond(odd == 0, together, apart, kv)
    q = exchange(q)

    def frame_of(index):
        return lax.dynamic_slice_in_dim(kv, index * FRAME, FRAME)

    def swap(block, low, high):
        pairs = [(a, a + 1) for a in range(low, high, 2)]
        return lax.ppermute(block, "slab", pairs + [(b, a) for a, b in pairs])

    far = swap(frame_of(odd), 1, slabs - 1)
    near = swap(frame_of(1 - odd), 0, slabs)
    far_present = ((slab > 0) & (slab < slabs - 1)).astype(jnp.int32)
    sums = attend_own(windows, q, kv)
    result = attend_halo(jnp.stack([1 - odd, 1]), windows, q, near, sums, NEAR_COST)
    result = attend_halo(jnp.stack([odd, far_present]), windows, q, far, sums, FAR_COST, (result,))
    return merge_heads(exchange(result))


def solution(mesh):
    rows = P(("slab", "head"), None)
    return jax.shard_map(
        on_device,
        mesh=mesh,
        in_specs=(rows, rows, rows, P(), P(), P("head", None)),
        out_specs=rows,
        check_vma=False,
    )
```
